1024 devices in a mesh: dom: 16 (over y, x), grp: 64 (over z, core).
Axes of the slice: x: 4, y: 4, z: 32, core: 2. Of those that a mesh axis runs over, the one named last changes fastest.
Arguments:
- features: bfloat16 [262144, 256], P(('dom', 'grp')), may hold values from -6 to 6
- adjacency: bfloat16 [16384, 128, 128], P(('dom', 'grp')), may hold values from -0.1875 to 0.1875
- src_tile: int32 [16384], P(('dom', 'grp')), may hold values from 0 to 1
- dst_peer: int32 [16384, 1], P(('dom', 'grp')), may hold values from 0 to 15; in each aligned block of 16 rows (0 to 15, 16 to 31, ...) at most 2 rows name the same one
- dst_tile: int32 [16384], P(('dom', 'grp')), may hold values from 0 to 1
- w_self: bfloat16 [256, 256], replicated, may hold values from -0.375 to 0.375
- w_neigh: bfloat16 [256, 256], replicated, may hold values from -0.375 to 0.375
- out_grad: bfloat16 [262144, 256], P(('dom', 'grp')), may hold values from -6 to 6
Outputs:
- output: bfloat16 [262144, 256], P(('dom', 'grp'))
- feat_grad: bfloat16 [262144, 256], P(('dom', 'grp'))
- weight_grads: float32 [2, 256, 256], replicated
The draws below stay inside these ranges and needn't reach their ends.
Inputs may be any that keep to these rules, and one draw needn't show every extreme that they name: `dst_peer`: among the 16 blocks of one device no partition is named more than 2 times, a bound that some block reaches.
All inputs are finite; a program needn't handle non-finite values.
Results may differ from the reference program's by a relative error of at most 0.015.
Values may be sent and summed in bfloat16 or wider, within the bound.
No kernel may reach another device: no remote copies, remote signals or barrier semaphores. Data moves between devices by JAX's collectives and lax.ppermute only.
A program may use at most 32 MiB of HBM per device.

```python
import math
import jax
import jax.numpy as jnp
import numpy as np
from jax import lax

F = 256
TILE = 128
TILES_DEV = 16
NT = 2
CAP = 2
NODES = 262144
TILES = 16384
N_DOM = 16
N_GRP = 64
DEVICES = 1024


def touch_ends(values, rng, low, high):
    place = [jax.random.randint(jax.random.fold_in(rng, axis), (), 0, length) for axis, length in enumerate(values.shape)]
    main_axis = values.shape.index(max(values.shape))
    beside = place[:main_axis] + [(place[main_axis] + 1) % values.shape[main_axis]] + place[main_axis + 1:]
    return values.at[tuple(place)].set(low).at[tuple(beside)].set(high)


def level_of(own_key, dims, pieces, least, high):
    def one(dim, blocks):
        heights = jax.random.uniform(jax.random.fold_in(jax.random.fold_in(own_key, 6), dim), (blocks,), jnp.float32, least / len(pieces), high / len(pieces))
        return jnp.repeat(jnp.exp(heights), dims[dim] // blocks).reshape((-1,) + (1,) * (len(dims) - dim - 1))

    gain = one(*pieces[0])
    for cut in pieces[1:]:
        gain = gain * one(*cut)
    return gain


def routed_block(key, own, number, rows, count, top, limit, slope):
    order = jax.random.permutation(key, count)
    crowded, ordinary = load_shares(count, rows * top, limit, slope, True), load_shares(count, rows * top, limit, slope, False)
    places = jnp.arange(count)

    def named(tallies, turn):
        used = int((tallies > 0).sum())
        fixed = max(1, used // 4)
        moved = fixed + (places - fixed + turn * (used - fixed)) % max(1, count - fixed)
        return jnp.zeros((count,), jnp.int32).at[order[jnp.where(places < fixed, places, moved)]].set(jnp.asarray(tallies, jnp.int32))

    tallies = jnp.where(number % 4 == 0, named(crowded, number // 4), named(ordinary, number - number // 4 - 1))
    mixed = jax.random.permutation(jax.random.fold_in(own, 3), count)
    source_of, receiver = mixed[0:count // 2 * 2:2], mixed[1:count // 2 * 2:2]
    margin = jnp.minimum(tallies[source_of] - 1, limit - tallies[receiver]) // 2
    margin = jnp.where((source_of == order[0]) | (receiver == order[0]) | (tallies[receiver] == 0), 0, jnp.maximum(margin, 0))
    moved = jax.random.randint(jax.random.fold_in(own, 4), (count // 2,), 0, 1 << 20) % (margin + 1)
    tallies = tallies.at[source_of].add(-moved).at[receiver].add(moved)
    members = jnp.searchsorted(jnp.cumsum(tallies), jnp.arange(rows * top), side="right").astype(jnp.int32)
    table = members.reshape(top, rows).T
    table = table[jax.random.permutation(jax.random.fold_in(own, 1), rows)]
    turn = jax.random.randint(jax.random.fold_in(own, 2), (rows, 1), 0, top)
    return jnp.take_along_axis(table, (jnp.arange(top)[None, :] + turn) % top, axis=1)


def load_shares(amount, total, bound, skew, full):
    weights = [(1 << 20) // math.isqrt(grade ** skew) + 1 for grade in range(1, amount + 1)]
    largest = bound if full else min(bound, max(-(-total // amount), total * weights[0] // sum(weights)))
    least = 1 if total - largest >= amount - 1 else 0
    given, rest = [largest] + [least] * (amount - 1), total - largest - least * (amount - 1)
    while rest > 0:
        candidates = [i for i in range(1, amount) if given[i] < largest] or [i for i in range(1, amount) if given[i] < bound]
        mass, remaining = sum([weights[i] for i in candidates]), rest
        for i in candidates:
            more = min(bound - given[i], max(1, remaining * weights[i] // mass), rest)
            given[i] = given[i] + more
            rest = rest - more
    return np.array(given)


def centred(own_key, extent, scale, limit, pieces=(), held_as=jnp.bfloat16):
    factor_of = level_of(own_key, extent, pieces, -0.22, 0.18) if pieces else 1.0
    entries = jax.random.normal(own_key, extent, jnp.float32) * scale * factor_of
    return jnp.minimum(jnp.maximum(entries, -limit), limit).astype(held_as)


def setup_inputs(seed: int = 0) -> dict:
    splits = jax.random.split(jax.random.key(seed), 9)
    features = centred(splits[0], (NODES, F), 1.0, 6.0, ((0, 1024),))
    adjacency = centred(splits[1], (TILES, TILE, TILE), (TILE * TILES_DEV // NT) ** -0.5, 0.1875, ((0, 1024),))
    src_tile = touch_ends(jax.random.randint(splits[2], (TILES,), 0, NT), jax.random.fold_in(splits[2], 1), 0, NT - 1).astype(jnp.int32)
    dst_peer_keys = jax.random.split(jax.random.fold_in(splits[3], 1), TILES // TILES_DEV)
    dst_peer_turns = jax.random.permutation(jax.random.fold_in(splits[3], 3), TILES // TILES_DEV)
    dst_peer = jax.vmap(lambda own, number: routed_block(jax.random.fold_in(splits[3], 2), own, number, TILES_DEV, N_DOM, 1, CAP, 2))(dst_peer_keys, dst_peer_turns).reshape((TILES, 1))
    dst_tile = touch_ends(jax.random.randint(splits[4], (TILES,), 0, NT), jax.random.fold_in(splits[4], 1), 0, NT - 1).astype(jnp.int32)
    w_self = centred(splits[5], (F, F), F ** -0.5, 0.375)
    w_neigh = centred(splits[6], (F, F), F ** -0.5, 0.375)
    out_grad = centred(splits[7], (NODES, F), 1.0, 6.0, ((0, 1024),))
    return {"features": features, "adjacency": adjacency, "src_tile": src_tile, "dst_peer": dst_peer, "dst_tile": dst_tile, "w_self": w_self, "w_neigh": w_neigh, "out_grad": out_grad}


def reference(features, adjacency, src_tile, dst_peer, dst_tile, w_self, w_neigh, out_grad):
    n_blocks = NODES // TILE
    device = jnp.arange(DEVICES, dtype=jnp.int32)
    group = device % N_GRP
    src_index = (device[:, None] * NT + src_tile.reshape(DEVICES, TILES_DEV)).astype(jnp.int32)
    dst_index = ((dst_peer[:, 0].reshape(DEVICES, TILES_DEV) * N_GRP + group[:, None]) * NT + dst_tile.reshape(DEVICES, TILES_DEV)).astype(jnp.int32)
    tiles = adjacency.reshape(DEVICES, TILES_DEV, TILE, TILE)
    blocks = features.reshape(n_blocks, TILE, F)

    def forward_step(carry, item):
        adj, src, dst = item
        prod = jnp.einsum('tij,tjf->tif', adj.astype(jnp.float32), blocks[src].astype(jnp.float32)).astype(jnp.bfloat16)
        return (carry.at[dst].add(prod.astype(jnp.float32)), None)
    agg, _ = lax.scan(forward_step, jnp.zeros((n_blocks, TILE, F), jnp.float32), (tiles, src_index, dst_index))
    agg_low = agg.reshape(NODES, F).astype(jnp.bfloat16)
    pre = jnp.dot(features, w_self, preferred_element_type=jnp.float32) + jnp.dot(agg_low, w_neigh, preferred_element_type=jnp.float32)
    sig = jax.nn.sigmoid(pre)
    output = (pre * sig).astype(jnp.bfloat16)
    dpre = (out_grad.astype(jnp.float32) * sig * (1.0 + pre * (1.0 - sig))).astype(jnp.bfloat16)
    scale = 1.0 / math.sqrt(NODES)
    grad_self = jnp.dot(features.T, dpre, preferred_element_type=jnp.float32) * scale
    grad_neigh = jnp.dot(agg_low.T, dpre, preferred_element_type=jnp.float32) * scale
    agg_grad = jnp.dot(dpre, w_neigh.T, preferred_element_type=jnp.float32).astype(jnp.bfloat16)
    grad_blocks = agg_grad.reshape(n_blocks, TILE, F)

    def backward_step(carry, item):
        adj, src, dst = item
        back = jnp.einsum('tij,tif->tjf', adj.astype(jnp.float32), grad_blocks[dst].astype(jnp.float32))
        return (carry.at[src].add(back), None)
    spread, _ = lax.scan(backward_step, jnp.zeros((n_blocks, TILE, F), jnp.float32), (tiles, src_index, dst_index))
    feat_grad = (jnp.dot(dpre, w_self.T, preferred_element_type=jnp.float32) + spread.reshape(NODES, F)).astype(jnp.bfloat16)
    return (output, feat_grad, jnp.stack([grad_self, grad_neigh]))
```

```python
import math

import jax
import jax.numpy as jnp
from jax import lax
from jax.experimental import pallas as pl
from jax.experimental.pallas import tpu as pltpu
from jax.sharding import Mesh
from jax.sharding import PartitionSpec as P

F32 = jnp.float32
BF16 = jnp.bfloat16
Z_LO = 2
LINE = ("y", "x")
NEAR = ("y", "x", "z_lo", "core")
FAR = "z_hi"
ALL = ("y", "x", "z_hi", "z_lo", "core")
TN = (((0,), (0,)), ((), ()))
NT = (((1,), (1,)), ((), ()))
LIMIT = 32 * 1024 * 1024


def smem():
    return pl.BlockSpec(memory_space=pltpu.SMEM)


def vmem():
    return pl.BlockSpec(memory_space=pltpu.VMEM)


def call(kernel, outs, n_smem, n_vmem, scratch=(), flops=0, size=0):
    return pl.pallas_call(
        kernel,
        out_shape=outs,
        in_specs=[smem()] * n_smem + [vmem()] * n_vmem,
        out_specs=jax.tree.map(lambda _: vmem(), outs),
        scratch_shapes=list(scratch),
        compiler_params=pltpu.CompilerParams(vmem_limit_bytes=LIMIT),
        cost_estimate=pl.CostEstimate(flops=flops, bytes_accessed=size, transcendentals=0),
    )


def shape(dims, dtype):
    return jax.ShapeDtypeStruct(dims, dtype)


def partial_sums(src_ref, peer_ref, dst_ref, feat_ref, adj_ref, out_ref):
    count, tile, _ = adj_ref.shape
    out_ref[...] = jnp.zeros_like(out_ref)
    for t in range(count):
        src = pl.multiple_of(src_ref[t] * tile, tile)
        dst = pl.multiple_of(dst_ref[t] * tile, tile)
        prod = jnp.dot(adj_ref[t], feat_ref[pl.ds(src, tile), :], preferred_element_type=F32)
        where = (peer_ref[t, 0], pl.ds(dst, tile), slice(None))
        out_ref[where] = (out_ref[where].astype(F32) + prod.astype(BF16).astype(F32)).astype(BF16)


def layer(recv_ref, feat_ref, ws_ref, wn_ref, grad_ref, out_ref, base_ref, agg_grad_ref, wg_ref):
    peers, nodes, width = recv_ref.shape
    agg = recv_ref[0].astype(F32)
    for p in range(1, peers):
        agg = agg + recv_ref[p].astype(F32)
    low = agg.astype(BF16)
    feat = feat_ref[...]
    pre = jnp.dot(feat, ws_ref[...], preferred_element_type=F32) + jnp.dot(
        low, wn_ref[...], preferred_element_type=F32
    )
    sig = jax.nn.sigmoid(pre)
    out_ref[...] = (pre * sig).astype(BF16)
    dpre = (grad_ref[...].astype(F32) * sig * (1.0 + pre * (1.0 - sig))).astype(BF16)
    chunks, rows, lanes = wg_ref.shape
    half = chunks // 2
    for k, left in enumerate((feat, low)):
        part = lax.dot_general(left, dpre, TN, preferred_element_type=F32)
        part = part.reshape(half, rows // 2, width)
        part = jnp.concatenate([part[:, :, :lanes], part[:, :, lanes:]], axis=1)
        wg_ref[k * half : (k + 1) * half] = part.astype(BF16)
    agg_grad = lax.dot_general(dpre, wn_ref[...], NT, preferred_element_type=F32).astype(BF16)
    for p in range(peers):
        agg_grad_ref[p] = agg_grad
    base_ref[...] = lax.dot_general(dpre, ws_ref[...], NT, preferred_element_type=F32)


def gradient(src_ref, peer_ref, dst_ref, adj_ref, every_ref, base_ref, out_ref, acc_ref):
    count, tile, _ = adj_ref.shape
    acc_ref[...] = base_ref[...]
    for t in range(count):
        src = pl.multiple_of(src_ref[t] * tile, tile)
        dst = pl.multiple_of(dst_ref[t] * tile, tile)
        picked = every_ref[peer_ref[t, 0], pl.ds(dst, tile), :]
        acc_ref[pl.ds(src, tile), :] += lax.dot_general(
            adj_ref[t], picked, TN, preferred_element_type=F32
        )
    out_ref[...] = acc_ref[...].astype(BF16)


def spread_sum(in_ref, out_ref):
    total = jnp.sum(in_ref[...].astype(F32), axis=0).astype(out_ref.dtype)
    for p in range(out_ref.shape[0]):
        out_ref[p] = total


def unpack(in_ref, out_ref, *, scale):
    got = in_ref[...].astype(F32) * scale
    chunks, rows, lanes = got.shape
    got = jnp.concatenate([got[:, : rows // 2], got[:, rows // 2 :]], axis=2)
    out_ref[...] = got.reshape(out_ref.shape)


def body(features, adjacency, src_tile, dst_peer, dst_tile, w_self, w_neigh, out_grad):
    nodes, width = features.shape
    count, tile, _ = adjacency.shape
    parts = lax.axis_size(LINE)
    near, far = lax.axis_size(NEAR), lax.axis_size(FAR)
    total_nodes = nodes * lax.axis_size(ALL)
    rows = 2 * width * width // near // 128
    dense = call(
        partial_sums,
        shape((parts, nodes, width), BF16),
        3,
        2,
        flops=2 * count * tile * tile * width,
        size=3 << 20,
    )(src_tile, dst_peer, dst_tile, features, adjacency)
    recv = lax.all_to_all(dense, LINE, 0, 0)
    output, base, mine, wgrad = call(
        layer,
        (
            shape((nodes, width), BF16),
            shape((nodes, width), F32),
            shape((parts, nodes, width), BF16),
            shape((near, rows, 128), BF16),
        ),
        0,
        5,
        flops=12 * nodes * width * width,
        size=5 << 20,
    )(recv, features, w_self, w_neigh, out_grad)
    wgrad = lax.all_to_all(wgrad, NEAR, 0, 0)
    wgrad = call(spread_sum, shape((far, rows, 128), BF16), 0, 1, size=1 << 19)(wgrad)
    every = lax.all_to_all(mine, LINE, 0, 0)
    wgrad = lax.all_to_all(wgrad, FAR, 0, 0)
    wgrad = call(spread_sum, shape((near, rows, 128), BF16), 0, 1, size=1 << 19)(wgrad)
    wgrad = lax.all_to_all(wgrad, NEAR, 0, 0)
    feat_grad = call(
        gradient,
        shape((nodes, width), BF16),
        3,
        3,
        scratch=[pltpu.VMEM((nodes, width), F32)],
        flops=2 * count * tile * tile * width,
        size=3 << 20,
    )(src_tile, dst_peer, dst_tile, adjacency, every, base)

    def last(in_ref, out_ref):
        unpack(in_ref, out_ref, scale=1.0 / math.sqrt(total_nodes))

    weight_grads = call(last, shape((2, width, width), F32), 0, 1, size=1 << 20)(wgrad)
    return (output, feat_grad, weight_grads)


def solution(mesh):
    dom, grp = mesh.devices.shape
    side = math.isqrt(dom)
    fine = Mesh(
        mesh.devices.reshape(side, dom // side, grp // (2 * Z_LO), Z_LO, 2), ALL
    )
    rows = P(ALL, None)
    in_specs = (rows, P(ALL, None, None), P(ALL), rows, P(ALL), P(), P(), rows)
    out_specs = (rows, rows, P())
    return jax.shard_map(body, mesh=fine, in_specs=in_specs, out_specs=out_specs, check_vma=False)
```

```python
import math

import jax
import jax.numpy as jnp
from jax import lax
from jax.experimental import pallas as pl
from jax.experimental.pallas import tpu as pltpu
from jax.sharding import Mesh
from jax.sharding import PartitionSpec as P

F32 = jnp.float32
BF16 = jnp.bfloat16
Z_LO = 2
LINE = ("y", "x")
NEAR = ("y", "x", "z_lo", "core")
FAR = "z_hi"
ALL = ("y", "x", "z_hi", "z_lo", "core")
TN = (((0,), (0,)), ((), ()))
NT = (((1,), (1,)), ((), ()))
LIMIT = 32 * 1024 * 1024


def smem():
    return pl.BlockSpec(memory_space=pltpu.SMEM)


def vmem():
    return pl.BlockSpec(memory_space=pltpu.VMEM)


def call(kernel, outs, n_smem, n_vmem, scratch=(), flops=0, size=0):
    return pl.pallas_call(
        kernel,
        out_shape=outs,
        in_specs=[smem()] * n_smem + [vmem()] * n_vmem,
        out_specs=jax.tree.map(lambda _: vmem(), outs),
        scratch_shapes=list(scratch),
        compiler_params=pltpu.CompilerParams(vmem_limit_bytes=LIMIT),
        cost_estimate=pl.CostEstimate(flops=flops, bytes_accessed=size, transcendentals=0),
    )


def shape(dims, dtype):
    return jax.ShapeDtypeStruct(dims, dtype)


def partial_sums(src_ref, peer_ref, dst_ref, feat_ref, adj_ref, out_ref):
    count, tile, _ = adj_ref.shape
    out_ref[...] = jnp.zeros_like(out_ref)
    for t in range(count):
        src = pl.multiple_of(src_ref[t] * tile, tile)
        dst = pl.multiple_of(dst_ref[t] * tile, tile)
        prod = jnp.dot(adj_ref[t], feat_ref[pl.ds(src, tile), :], preferred_element_type=F32)
        where = (peer_ref[t], pl.ds(dst, tile), slice(None))
        out_ref[where] = (out_ref[where].astype(F32) + prod.astype(BF16).astype(F32)).astype(BF16)


def layer(recv_ref, feat_ref, ws_ref, wn_ref, grad_ref, out_ref, base_ref, agg_grad_ref, wg_ref):
    peers, nodes, width = recv_ref.shape
    agg = recv_ref[0].astype(F32)
    for p in range(1, peers):
        agg = agg + recv_ref[p].astype(F32)
    low = agg.astype(BF16)
    feat = feat_ref[...]
    pre = jnp.dot(feat, ws_ref[...], preferred_element_type=F32) + jnp.dot(
        low, wn_ref[...], preferred_element_type=F32
    )
    sig = jax.nn.sigmoid(pre)
    out_ref[...] = (pre * sig).astype(BF16)
    dpre = (grad_ref[...].astype(F32) * sig * (1.0 + pre * (1.0 - sig))).astype(BF16)
    chunks, rows, lanes = wg_ref.shape
    half = chunks // 2
    for k, left in enumerate((feat, low)):
        part = lax.dot_general(left, dpre, TN, preferred_element_type=F32)
        part = part.reshape(half, rows // 2, width)
        part = jnp.concatenate([part[:, :, :lanes], part[:, :, lanes:]], axis=1)
        wg_ref[k * half : (k + 1) * half] = part.astype(BF16)
    agg_grad_ref[...] = lax.dot_general(
        dpre, wn_ref[...], NT, preferred_element_type=F32
    ).astype(BF16)
    base_ref[...] = lax.dot_general(dpre, ws_ref[...], NT, preferred_element_type=F32)


def gradient(
    src_ref, peer_ref, dst_ref, adj_ref, base_ref, s0, s1, s2, s3, out_ref, acc_ref, every_ref
):
    count, tile, _ = adj_ref.shape
    wide = s0.shape[0]
    for k, stack in enumerate((s0, s1, s2, s3)):
        every_ref[k * wide : (k + 1) * wide] = stack[...]
    acc_ref[...] = base_ref[...]
    for t in range(count):
        src = pl.multiple_of(src_ref[t] * tile, tile)
        dst = pl.multiple_of(dst_ref[t] * tile, tile)
        picked = every_ref[peer_ref[t], pl.ds(dst, tile), :]
        acc_ref[pl.ds(src, tile), :] += lax.dot_general(
            adj_ref[t], picked, TN, preferred_element_type=F32
        )
    out_ref[...] = acc_ref[...].astype(BF16)


def spread_sum(in_ref, out_ref):
    total = jnp.sum(in_ref[...].astype(F32), axis=0).astype(out_ref.dtype)
    for p in range(out_ref.shape[0]):
        out_ref[p] = total


def unpack(in_ref, out_ref, *, scale):
    got = in_ref[...].astype(F32) * scale
    chunks, rows, lanes = got.shape
    got = jnp.concatenate([got[:, : rows // 2], got[:, rows // 2 :]], axis=2)
    out_ref[...] = got.reshape(out_ref.shape)


def from_ahead(value, axis, step):
    n = lax.axis_size(axis)
    return lax.ppermute(value, axis, [((i + step) % n, i) for i in range(n)])


def body(features, adjacency, src_tile, dst_peer, dst_tile, w_self, w_neigh, out_grad):
    nodes, width = features.shape
    count, tile, _ = adjacency.shape
    parts = lax.axis_size(LINE)
    near, far = lax.axis_size(NEAR), lax.axis_size(FAR)
    total_nodes = nodes * lax.axis_size(ALL)
    rows = 2 * width * width // near // 128
    peer = dst_peer.reshape(count)
    n_y, n_x = lax.axis_size("y"), lax.axis_size("x")
    ahead = (peer // n_x - lax.axis_index("y")) % n_y * n_x + (
        peer % n_x - lax.axis_index("x")
    ) % n_x
    dense = call(
        partial_sums,
        shape((parts, nodes, width), BF16),
        3,
        2,
        flops=2 * count * tile * tile * width,
        size=3 << 20,
    )(src_tile, peer, dst_tile, features, adjacency)
    recv = lax.all_to_all(dense, LINE, 0, 0)
    output, base, mine, wgrad = call(
        layer,
        (
            shape((nodes, width), BF16),
            shape((nodes, width), F32),
            shape((nodes, width), BF16),
            shape((near, rows, 128), BF16),
        ),
        0,
        5,
        flops=12 * nodes * width * width,
        size=5 << 20,
    )(recv, features, w_self, w_neigh, out_grad)
    wgrad = lax.all_to_all(wgrad, NEAR, 0, 0)
    line = [mine] + [from_ahead(mine, "x", k) for k in range(1, n_x)]
    wgrad, line = lax.optimization_barrier((wgrad, line))
    wgrad = call(spread_sum, shape((far, rows, 128), BF16), 0, 1, size=1 << 19)(wgrad)
    wgrad = lax.all_to_all(wgrad, FAR, 0, 0)
    line = jnp.stack(line)
    stacks = [line] + [from_ahead(line, "y", k) for k in range(1, n_y)]
    wgrad, stacks = lax.optimization_barrier((wgrad, stacks))
    wgrad = call(spread_sum, shape((near, rows, 128), BF16), 0, 1, size=1 << 19)(wgrad)
    wgrad = lax.all_to_all(wgrad, NEAR, 0, 0)
    feat_grad = call(
        gradient,
        shape((nodes, width), BF16),
        3,
        2 + n_y,
        scratch=[pltpu.VMEM((nodes, width), F32), pltpu.VMEM((parts, nodes, width), BF16)],
        flops=2 * count * tile * tile * width,
        size=3 << 20,
    )(src_tile, ahead, dst_tile, adjacency, base, *stacks)

    def last(in_ref, out_ref):
        unpack(in_ref, out_ref, scale=1.0 / math.sqrt(total_nodes))

    weight_grads = call(last, shape((2, width, width), F32), 0, 1, size=1 << 20)(wgrad)
    return (output, feat_grad, weight_grads)


def solution(mesh):
    dom, grp = mesh.devices.shape
    side = math.isqrt(dom)
    fine = Mesh(
        mesh.devices.reshape(side, dom // side, grp // (2 * Z_LO), Z_LO, 2), ALL
    )
    rows = P(ALL, None)
    in_specs = (rows, P(ALL, None, None), P(ALL), rows, P(ALL), P(), P(), rows)
    out_specs = (rows, rows, P())
    return jax.shard_map(body, mesh=fine, in_specs=in_specs, out_specs=out_specs, check_vma=False)
```

```python
import math

import jax
import jax.numpy as jnp
from jax import lax
from jax.experimental import pallas as pl
from jax.experimental.pallas import tpu as pltpu
from jax.sharding import Mesh
from jax.sharding import PartitionSpec as P

F32 = jnp.float32
BF16 = jnp.bfloat16
Z_LO = 2
LINE = ("y", "x")
NEAR = ("y", "x", "z_lo", "core")
REST = ("y", "z_lo", "core")
FAR = "z_hi"
ALL = ("y", "x", "z_hi", "z_lo", "core")
TN = (((0,), (0,)), ((), ()))
NT = (((1,), (1,)), ((), ()))
LIMIT = 32 * 1024 * 1024


def smem():
    return pl.BlockSpec(memory_space=pltpu.SMEM)


def vmem():
    return pl.BlockSpec(memory_space=pltpu.VMEM)


def call(kernel, outs, n_smem, n_vmem, scratch=(), flops=0, size=0):
    return pl.pallas_call(
        kernel,
        out_shape=outs,
        in_specs=[smem()] * n_smem + [vmem()] * n_vmem,
        out_specs=jax.tree.map(lambda _: vmem(), outs),
        scratch_shapes=list(scratch),
        compiler_params=pltpu.CompilerParams(vmem_limit_bytes=LIMIT),
        cost_estimate=pl.CostEstimate(flops=flops, bytes_accessed=size, transcendentals=0),
    )


def shape(dims, dtype):
    return jax.ShapeDtypeStruct(dims, dtype)


def partial_sums(
    src_in, peer_in, dst_in, feat_in, adj_in, out_ref, src_ref, peer_ref, dst_ref, feat_ref, adj_ref, sems
):
    pairs = ((src_in, src_ref), (peer_in, peer_ref), (dst_in, dst_ref), (feat_in, feat_ref), (adj_in, adj_ref))
    copies = [pltpu.make_async_copy(a, b, sems.at[k]) for k, (a, b) in enumerate(pairs)]
    for copy in reversed(copies):
        copy.start()
    count, tile, _ = adj_ref.shape
    out_ref[...] = jnp.zeros_like(out_ref)
    for copy in copies:
        copy.wait()
    for t in range(count):
        src = pl.multiple_of(src_ref[t] * tile, tile)
        dst = pl.multiple_of(dst_ref[t] * tile, tile)
        prod = jnp.dot(adj_ref[t], feat_ref[pl.ds(src, tile), :], preferred_element_type=F32)
        where = (peer_ref[t], pl.ds(dst, tile), slice(None))
        out_ref[where] = (out_ref[where].astype(F32) + prod.astype(BF16).astype(F32)).astype(BF16)


def layer(recv_ref, feat_ref, ws_ref, wn_ref, grad_ref, out_ref, base_ref, sent_ref):
    peers, nodes, width = recv_ref.shape
    agg = recv_ref[0].astype(F32)
    for p in range(1, peers):
        agg = agg + recv_ref[p].astype(F32)
    low = agg.astype(BF16)
    feat = feat_ref[...]
    pre = jnp.dot(feat, ws_ref[...], preferred_element_type=F32) + jnp.dot(
        low, wn_ref[...], preferred_element_type=F32
    )
    sig = jax.nn.sigmoid(pre)
    out_ref[...] = (pre * sig).astype(BF16)
    dpre = (grad_ref[...].astype(F32) * sig * (1.0 + pre * (1.0 - sig))).astype(BF16)
    agg_grad = lax.dot_general(dpre, wn_ref[...], NT, preferred_element_type=F32).astype(BF16)
    n_x, length, _ = sent_ref.shape
    share = (length - nodes) // (2 * 2)
    for k, left in enumerate((feat, low)):
        part = lax.dot_general(left, dpre, TN, preferred_element_type=F32).astype(BF16)
        part = part.reshape(2, n_x, share, width)
        for x in range(n_x):
            for y in range(2):
                at = nodes + (2 * k + y) * share
                sent_ref[x, at : at + share] = part[y, x]
    for x in range(n_x):
        sent_ref[x, :nodes] = agg_grad
    base_ref[...] = lax.dot_general(dpre, ws_ref[...], NT, preferred_element_type=F32)


def gradient(
    src_ref, peer_ref, dst_ref, adj_ref, base_ref, s0, s1, s2, s3, out_ref, acc_ref, every_ref
):
    count, tile, _ = adj_ref.shape
    wide = s0.shape[0]
    for k, stack in enumerate((s0, s1, s2, s3)):
        every_ref[k * wide : (k + 1) * wide] = stack[...]
    acc_ref[...] = base_ref[...]
    for t in range(count):
        src = pl.multiple_of(src_ref[t] * tile, tile)
        dst = pl.multiple_of(dst_ref[t] * tile, tile)
        picked = every_ref[peer_ref[t], pl.ds(dst, tile), :]
        acc_ref[pl.ds(src, tile), :] += lax.dot_general(
            adj_ref[t], picked, TN, preferred_element_type=F32
        )
    out_ref[...] = acc_ref[...].astype(BF16)


def split_line(in_ref, line_ref, wg_ref):
    nodes, width = line_ref.shape[1:]
    chunks, rows, lanes = wg_ref.shape
    line_ref[...] = in_ref[:, :nodes]
    part = jnp.sum(in_ref[:, nodes:].astype(F32), axis=0).reshape(chunks, rows // 2, width)
    wg_ref[...] = jnp.concatenate([part[:, :, :lanes], part[:, :, lanes:]], axis=1).astype(BF16)


def spread_sum(in_ref, out_ref):
    total = jnp.sum(in_ref[...].astype(F32), axis=0).astype(out_ref.dtype)
    for p in range(out_ref.shape[0]):
        out_ref[p] = total


def unpack(in_ref, out_ref, *, scale):
    got = in_ref[...].astype(F32) * scale
    chunks, rows, lanes = got.shape
    got = jnp.concatenate([got[:, : rows // 2], got[:, rows // 2 :]], axis=2)
    out_ref[...] = got.reshape(out_ref.shape)


def from_ahead(value, axis, step):
    n = lax.axis_size(axis)
    return lax.ppermute(value, axis, [((i + step) % n, i) for i in range(n)])


def body(features, adjacency, src_tile, dst_peer, dst_tile, w_self, w_neigh, out_grad):
    nodes, width = features.shape
    count, tile, _ = adjacency.shape
    parts = lax.axis_size(LINE)
    near, far = lax.axis_size(NEAR), lax.axis_size(FAR)
    total_nodes = nodes * lax.axis_size(ALL)
    rows = 2 * width * width // near // 128
    peer = dst_peer.reshape(count)
    n_y, n_x = lax.axis_size("y"), lax.axis_size("x")
    ahead = (peer // n_x - lax.axis_index("y")) % n_y * n_x + peer % n_x
    dense = pl.pallas_call(
        partial_sums,
        out_shape=shape((parts, nodes, width), BF16),
        in_specs=[pl.BlockSpec(memory_space=pltpu.HBM)] * 5,
        out_specs=vmem(),
        scratch_shapes=[pltpu.SMEM((count,), jnp.int32)] * 3
        + [pltpu.VMEM((nodes, width), BF16), pltpu.VMEM((count, tile, tile), BF16)]
        + [pltpu.SemaphoreType.DMA((5,))],
        compiler_params=pltpu.CompilerParams(vmem_limit_bytes=60 << 20),
        cost_estimate=pl.CostEstimate(
            flops=2 * count * tile * tile * width, bytes_accessed=3 << 20, transcendentals=0
        ),
    )(src_tile, peer, dst_tile, features, adjacency)
    recv = lax.all_to_all(dense, LINE, 0, 0)
    output, base, sent = call(
        layer,
        (
            shape((nodes, width), BF16),
            shape((nodes, width), F32),
            shape((n_x, nodes + 2 * width // n_x, width), BF16),
        ),
        0,
        5,
        flops=12 * nodes * width * width,
        size=5 << 20,
    )(recv, features, w_self, w_neigh, out_grad)
    sent = lax.all_to_all(sent, "x", 0, 0)
    line, wgrad = call(
        split_line,
        (shape((n_x, nodes, width), BF16), shape((near // n_x, rows, 128), BF16)),
        0,
        1,
        size=1 << 20,
    )(sent)
    wgrad = lax.all_to_all(wgrad, REST, 0, 0)
    stacks = [line] + [from_ahead(line, "y", k) for k in range(1, n_y)]
    wgrad = call(spread_sum, shape((far, rows, 128), BF16), 0, 1, size=1 << 19)(wgrad)
    wgrad = lax.all_to_all(wgrad, FAR, 0, 0)
    wgrad, stacks = lax.optimization_barrier((wgrad, stacks))
    wgrad = call(spread_sum, shape((near, rows, 128), BF16), 0, 1, size=1 << 19)(wgrad)
    wgrad = lax.all_to_all(wgrad, NEAR, 0, 0)
    feat_grad = call(
        gradient,
        shape((nodes, width), BF16),
        3,
        2 + n_y,
        scratch=[pltpu.VMEM((nodes, width), F32), pltpu.VMEM((parts, nodes, width), BF16)],
        flops=2 * count * tile * tile * width,
        size=3 << 20,
    )(src_tile, ahead, dst_tile, adjacency, base, *stacks)

    def last(in_ref, out_ref):
        unpack(in_ref, out_ref, scale=1.0 / math.sqrt(total_nodes))

    weight_grads = call(last, shape((2, width, width), F32), 0, 1, size=1 << 20)(wgrad)
    return (output, feat_grad, weight_grads)


def solution(mesh):
    dom, grp = mesh.devices.shape
    side = math.isqrt(dom)
    fine = Mesh(
        mesh.devices.reshape(side, dom // side, grp // (2 * Z_LO), Z_LO, 2), ALL
    )
    rows = P(ALL, None)
    in_specs = (rows, P(ALL, None, None), P(ALL), rows, P(ALL), P(), P(), rows)
    out_specs = (rows, rows, P())
    return jax.shard_map(body, mesh=fine, in_specs=in_specs, out_specs=out_specs, check_vma=False)
```

```python
import functools
import math

import jax
import jax.numpy as jnp
from jax import lax
from jax.experimental import pallas as pl
from jax.experimental.pallas import tpu as pltpu
from jax.sharding import Mesh
from jax.sharding import PartitionSpec as P

F32 = jnp.float32
BF16 = jnp.bfloat16
Z_LO = 2
LINE = ("y", "x")
NEAR = ("y", "x", "z_lo", "core")
REST = ("y", "z_lo", "core")
FAR = "z_hi"
ALL = ("y", "x", "z_hi", "z_lo", "core")
TN = (((0,), (0,)), ((), ()))
NT = (((1,), (1,)), ((), ()))
LIMIT = 32 * 1024 * 1024


def smem():
    return pl.BlockSpec(memory_space=pltpu.SMEM)


def vmem():
    return pl.BlockSpec(memory_space=pltpu.VMEM)


def call(kernel, outs, n_smem, n_vmem, scratch=(), flops=0, size=0):
    return pl.pallas_call(
        kernel,
        out_shape=outs,
        in_specs=[smem()] * n_smem + [vmem()] * n_vmem,
        out_specs=jax.tree.map(lambda _: vmem(), outs),
        scratch_shapes=list(scratch),
        compiler_params=pltpu.CompilerParams(vmem_limit_bytes=LIMIT),
        cost_estimate=pl.CostEstimate(flops=flops, bytes_accessed=size, transcendentals=0),
    )


def shape(dims, dtype):
    return jax.ShapeDtypeStruct(dims, dtype)


def partial_sums(
    src_in, peer_in, dst_in, feat_in, adj_in, out_ref, src_ref, peer_ref, dst_ref, feat_ref, adj_ref, sems, *, lead
):
    parts = out_ref.shape[0]
    pairs = ((src_in, src_ref), (peer_in, peer_ref), (dst_in, dst_ref), (feat_in, feat_ref), (adj_in, adj_ref))
    copies = [pltpu.make_async_copy(a, b, sems.at[k]) for k, (a, b) in enumerate(pairs)]
    for copy in reversed(copies):
        copy.start()
    count, tile, _ = adj_ref.shape
    out_ref[...] = jnp.zeros_like(out_ref)
    for copy in copies:
        copy.wait()
    for t in range(count):
        src = pl.multiple_of(src_ref[t] * tile, tile)
        dst = pl.multiple_of(dst_ref[t] * tile, tile)
        prod = jnp.dot(adj_ref[t], feat_ref[pl.ds(src, tile), :], preferred_element_type=F32)
        where = (lax.rem(peer_ref[t] + (parts - lead), parts), pl.ds(dst, tile), slice(None))
        out_ref[where] = (out_ref[where].astype(F32) + prod.astype(BF16).astype(F32)).astype(BF16)


def layer(recv_ref, feat_ref, ws_ref, wn_ref, grad_ref, out_ref, base_ref, sent_ref):
    peers, nodes, width = recv_ref.shape
    agg = recv_ref[0].astype(F32)
    for p in range(1, peers):
        agg = agg + recv_ref[p].astype(F32)
    low = agg.astype(BF16)
    feat = feat_ref[...]
    pre = jnp.dot(feat, ws_ref[...], preferred_element_type=F32) + jnp.dot(
        low, wn_ref[...], preferred_element_type=F32
    )
    sig = jax.nn.sigmoid(pre)
    out_ref[...] = (pre * sig).astype(BF16)
    dpre = (grad_ref[...].astype(F32) * sig * (1.0 + pre * (1.0 - sig))).astype(BF16)
    agg_grad = lax.dot_general(dpre, wn_ref[...], NT, preferred_element_type=F32).astype(BF16)
    n_x, length, _ = sent_ref.shape
    share = (length - nodes) // (2 * 2)
    for k, left in enumerate((feat, low)):
        part = lax.dot_general(left, dpre, TN, preferred_element_type=F32).astype(BF16)
        part = part.reshape(2, n_x, share, width)
        for x in range(n_x):
            for y in range(2):
                at = nodes + (2 * k + y) * share
                sent_ref[x, at : at + share] = part[y, x]
    for x in range(n_x):
        sent_ref[x, :nodes] = agg_grad
    base_ref[...] = lax.dot_general(dpre, ws_ref[...], NT, preferred_element_type=F32)


def gradient(
    src_ref, peer_ref, dst_ref, adj_ref, base_ref, s0, s1, s2, s3, out_ref, acc_ref, every_ref
):
    count, tile, _ = adj_ref.shape
    wide = s0.shape[0]
    for k, stack in enumerate((s0, s1, s2, s3)):
        every_ref[k * wide : (k + 1) * wide] = stack[...]
    acc_ref[...] = base_ref[...]
    for t in range(count):
        src = pl.multiple_of(src_ref[t] * tile, tile)
        dst = pl.multiple_of(dst_ref[t] * tile, tile)
        picked = every_ref[peer_ref[t], pl.ds(dst, tile), :]
        acc_ref[pl.ds(src, tile), :] += lax.dot_general(
            adj_ref[t], picked, TN, preferred_element_type=F32
        )
    out_ref[...] = acc_ref[...].astype(BF16)


def split_line(in_ref, line_ref, wg_ref):
    nodes, width = line_ref.shape[1:]
    chunks, rows, lanes = wg_ref.shape
    line_ref[...] = in_ref[:, :nodes]
    part = jnp.sum(in_ref[:, nodes:].astype(F32), axis=0).reshape(chunks, rows // 2, width)
    wg_ref[...] = jnp.concatenate([part[:, :, :lanes], part[:, :, lanes:]], axis=1).astype(BF16)


def spread_sum(in_ref, out_ref):
    total = jnp.sum(in_ref[...].astype(F32), axis=0).astype(out_ref.dtype)
    for p in range(out_ref.shape[0]):
        out_ref[p] = total


def unpack(in_ref, out_ref, *, scale):
    got = in_ref[...].astype(F32) * scale
    chunks, rows, lanes = got.shape
    got = jnp.concatenate([got[:, : rows // 2], got[:, rows // 2 :]], axis=2)
    out_ref[...] = got.reshape(out_ref.shape)


def led_by(first, count):
    return [(first + k) % count for k in range(count)]


def from_ahead(value, axis, step):
    n = lax.axis_size(axis)
    return lax.ppermute(value, axis, [((i + step) % n, i) for i in range(n)])


def body(features, adjacency, src_tile, dst_peer, dst_tile, w_self, w_neigh, out_grad):
    nodes, width = features.shape
    count, tile, _ = adjacency.shape
    parts = lax.axis_size(LINE)
    near, far = lax.axis_size(NEAR), lax.axis_size(FAR)
    total_nodes = nodes * lax.axis_size(ALL)
    rows = 2 * width * width // near // 128
    peer = dst_peer.reshape(count)
    lead = parts * 10 // 16
    n_y, n_x = lax.axis_size("y"), lax.axis_size("x")
    ahead = (peer // n_x - lax.axis_index("y")) % n_y * n_x + peer % n_x
    dense = pl.pallas_call(
        functools.partial(partial_sums, lead=lead),
        out_shape=shape((parts, nodes, width), BF16),
        in_specs=[pl.BlockSpec(memory_space=pltpu.HBM)] * 5,
        out_specs=vmem(),
        scratch_shapes=[pltpu.SMEM((count,), jnp.int32)] * 3
        + [pltpu.VMEM((nodes, width), BF16), pltpu.VMEM((count, tile, tile), BF16)]
        + [pltpu.SemaphoreType.DMA((5,))],
        compiler_params=pltpu.CompilerParams(vmem_limit_bytes=60 << 20),
        cost_estimate=pl.CostEstimate(
            flops=2 * count * tile * tile * width, bytes_accessed=3 << 20, transcendentals=0
        ),
    )(src_tile, peer, dst_tile, features, adjacency)
    recv = lax.all_to_all(dense, LINE, 0, 0, axis_index_groups=[led_by(lead, parts)])
    output, base, sent = call(
        layer,
        (
            shape((nodes, width), BF16),
            shape((nodes, width), F32),
            shape((n_x, nodes + 2 * width // n_x, width), BF16),
        ),
        0,
        5,
        flops=12 * nodes * width * width,
        size=5 << 20,
    )(recv, features, w_self, w_neigh, out_grad)
    sent = lax.all_to_all(sent, "x", 0, 0)
    line, wgrad = call(
        split_line,
        (shape((n_x, nodes, width), BF16), shape((near // n_x, rows, 128), BF16)),
        0,
        1,
        size=1 << 20,
    )(sent)
    wgrad = lax.all_to_all(wgrad, REST, 0, 0)
    stacks = [line] + [from_ahead(line, "y", k) for k in range(1, n_y)]
    wgrad = call(spread_sum, shape((far, rows, 128), BF16), 0, 1, size=1 << 19)(wgrad)
    wgrad = lax.all_to_all(wgrad, FAR, 0, 0, axis_index_groups=[led_by(far * 10 // 16, far)])
    wgrad, stacks = lax.optimization_barrier((wgrad, stacks))
    wgrad = call(spread_sum, shape((near, rows, 128), BF16), 0, 1, size=1 << 19)(wgrad)
    wgrad = lax.all_to_all(wgrad, NEAR, 0, 0)
    feat_grad = call(
        gradient,
        shape((nodes, width), BF16),
        3,
        2 + n_y,
        scratch=[pltpu.VMEM((nodes, width), F32), pltpu.VMEM((parts, nodes, width), BF16)],
        flops=2 * count * tile * tile * width,
        size=3 << 20,
    )(src_tile, ahead, dst_tile, adjacency, base, *stacks)

    def last(in_ref, out_ref):
        unpack(in_ref, out_ref, scale=1.0 / math.sqrt(total_nodes))

    weight_grads = call(last, shape((2, width, width), F32), 0, 1, size=1 << 20)(wgrad)
    return (output, feat_grad, weight_grads)


def solution(mesh):
    dom, grp = mesh.devices.shape
    side = math.isqrt(dom)
    fine = Mesh(
        mesh.devices.reshape(side, dom // side, grp // (2 * Z_LO), Z_LO, 2), ALL
    )
    rows = P(ALL, None)
    in_specs = (rows, P(ALL, None, None), P(ALL), rows, P(ALL), P(), P(), rows)
    out_specs = (rows, rows, P())
    return jax.shard_map(body, mesh=fine, in_specs=in_specs, out_specs=out_specs, check_vma=False)
```

```python
import functools
import math

import jax
import jax.numpy as jnp
from jax import lax
from jax.experimental import pallas as pl
from jax.experimental.pallas import tpu as pltpu
from jax.sharding import Mesh
from jax.sharding import PartitionSpec as P

F32 = jnp.float32
BF16 = jnp.bfloat16
Z_LO = 2
LINE = ("y", "x")
NEAR = ("y", "x", "z_lo", "core")
FAR = "z_hi"
ALL = ("y", "x", "z_hi", "z_lo", "core")
TN = (((0,), (0,)), ((), ()))
NT = (((1,), (1,)), ((), ()))
LIMIT = 32 * 1024 * 1024


def smem():
    return pl.BlockSpec(memory_space=pltpu.SMEM)


def vmem():
    return pl.BlockSpec(memory_space=pltpu.VMEM)


def call(kernel, outs, n_smem, n_vmem, scratch=(), flops=0, size=0):
    return pl.pallas_call(
        kernel,
        out_shape=outs,
        in_specs=[smem()] * n_smem + [vmem()] * n_vmem,
        out_specs=jax.tree.map(lambda _: vmem(), outs),
        scratch_shapes=list(scratch),
        compiler_params=pltpu.CompilerParams(vmem_limit_bytes=LIMIT),
        cost_estimate=pl.CostEstimate(flops=flops, bytes_accessed=size, transcendentals=0),
    )


def shape(dims, dtype):
    return jax.ShapeDtypeStruct(dims, dtype)


def partial_sums(
    src_in, peer_in, dst_in, feat_in, adj_in, out_ref, src_ref, peer_ref, dst_ref, feat_ref, adj_ref, sems, *, lead
):
    parts = out_ref.shape[0]
    pairs = ((src_in, src_ref), (peer_in, peer_ref), (dst_in, dst_ref), (feat_in, feat_ref), (adj_in, adj_ref))
    copies = [pltpu.make_async_copy(a, b, sems.at[k]) for k, (a, b) in enumerate(pairs)]
    for copy in reversed(copies):
        copy.start()
    count, tile, _ = adj_ref.shape
    out_ref[...] = jnp.zeros_like(out_ref)
    for copy in copies:
        copy.wait()
    for t in range(count):
        src = pl.multiple_of(src_ref[t] * tile, tile)
        dst = pl.multiple_of(dst_ref[t] * tile, tile)
        prod = jnp.dot(adj_ref[t], feat_ref[pl.ds(src, tile), :], preferred_element_type=F32)
        where = (lax.rem(peer_ref[t] + (parts - lead), parts), pl.ds(dst, tile), slice(None))
        out_ref[where] = (out_ref[where].astype(F32) + prod.astype(BF16).astype(F32)).astype(BF16)


def layer(recv_ref, feat_ref, ws_ref, wn_ref, grad_ref, out_ref, base_ref, agg_grad_ref, wg_ref):
    peers, nodes, width = recv_ref.shape
    agg = recv_ref[0].astype(F32)
    for p in range(1, peers):
        agg = agg + recv_ref[p].astype(F32)
    low = agg.astype(BF16)
    feat = feat_ref[...]
    pre = jnp.dot(feat, ws_ref[...], preferred_element_type=F32) + jnp.dot(
        low, wn_ref[...], preferred_element_type=F32
    )
    sig = jax.nn.sigmoid(pre)
    out_ref[...] = (pre * sig).astype(BF16)
    dpre = (grad_ref[...].astype(F32) * sig * (1.0 + pre * (1.0 - sig))).astype(BF16)
    agg_grad = lax.dot_general(dpre, wn_ref[...], NT, preferred_element_type=F32).astype(BF16)
    for x in range(agg_grad_ref.shape[0]):
        agg_grad_ref[x] = agg_grad
    chunks, rows, lanes = wg_ref.shape
    half = chunks // 2
    for k, left in enumerate((feat, low)):
        part = lax.dot_general(left, dpre, TN, preferred_element_type=F32)
        part = part.reshape(half, rows // 2, width)
        part = jnp.concatenate([part[:, :, :lanes], part[:, :, lanes:]], axis=1)
        wg_ref[k * half : (k + 1) * half] = part.astype(BF16)
    base_ref[...] = lax.dot_general(dpre, ws_ref[...], NT, preferred_element_type=F32)


def gradient(
    src_ref, peer_ref, dst_ref, adj_ref, base_ref, s0, s1, s2, s3, out_ref, acc_ref, every_ref
):
    count, tile, _ = adj_ref.shape
    wide = s0.shape[0]
    for k, stack in enumerate((s0, s1, s2, s3)):
        every_ref[k * wide : (k + 1) * wide] = stack[...]
    acc_ref[...] = base_ref[...]
    for t in range(count):
        src = pl.multiple_of(src_ref[t] * tile, tile)
        dst = pl.multiple_of(dst_ref[t] * tile, tile)
        picked = every_ref[peer_ref[t], pl.ds(dst, tile), :]
        acc_ref[pl.ds(src, tile), :] += lax.dot_general(
            adj_ref[t], picked, TN, preferred_element_type=F32
        )
    out_ref[...] = acc_ref[...].astype(BF16)


def spread_sum(in_ref, out_ref):
    total = jnp.sum(in_ref[...].astype(F32), axis=0).astype(out_ref.dtype)
    for p in range(out_ref.shape[0]):
        out_ref[p] = total


def unpack(in_ref, out_ref, *, scale):
    got = in_ref[...].astype(F32) * scale
    chunks, rows, lanes = got.shape
    got = jnp.concatenate([got[:, : rows // 2], got[:, rows // 2 :]], axis=2)
    out_ref[...] = got.reshape(out_ref.shape)


def led_by(first, count):
    return [(first + k) % count for k in range(count)]


def from_ahead(value, axis, step):
    n = lax.axis_size(axis)
    return lax.ppermute(value, axis, [((i + step) % n, i) for i in range(n)])


def body(features, adjacency, src_tile, dst_peer, dst_tile, w_self, w_neigh, out_grad):
    nodes, width = features.shape
    count, tile, _ = adjacency.shape
    parts = lax.axis_size(LINE)
    near, far = lax.axis_size(NEAR), lax.axis_size(FAR)
    total_nodes = nodes * lax.axis_size(ALL)
    rows = 2 * width * width // near // 128
    peer = dst_peer.reshape(count)
    lead = parts * 10 // 16
    n_y, n_x = lax.axis_size("y"), lax.axis_size("x")
    ahead = (peer // n_x - lax.axis_index("y")) % n_y * n_x + peer % n_x
    dense = pl.pallas_call(
        functools.partial(partial_sums, lead=lead),
        out_shape=shape((parts, nodes, width), BF16),
        in_specs=[pl.BlockSpec(memory_space=pltpu.HBM)] * 5,
        out_specs=vmem(),
        scratch_shapes=[pltpu.SMEM((count,), jnp.int32)] * 3
        + [pltpu.VMEM((nodes, width), BF16), pltpu.VMEM((count, tile, tile), BF16)]
        + [pltpu.SemaphoreType.DMA((5,))],
        compiler_params=pltpu.CompilerParams(vmem_limit_bytes=60 << 20),
        cost_estimate=pl.CostEstimate(
            flops=2 * count * tile * tile * width, bytes_accessed=3 << 20, transcendentals=0
        ),
    )(src_tile, peer, dst_tile, features, adjacency)
    recv = lax.all_to_all(dense, LINE, 0, 0, axis_index_groups=[led_by(lead, parts)])
    output, base, line, wgrad = call(
        layer,
        (
            shape((nodes, width), BF16),
            shape((nodes, width), F32),
            shape((n_x, nodes, width), BF16),
            shape((near, rows, 128), BF16),
        ),
        0,
        5,
        flops=12 * nodes * width * width,
        size=5 << 20,
    )(recv, features, w_self, w_neigh, out_grad)
    line = lax.all_to_all(line, "x", 0, 0)
    line, wgrad = lax.optimization_barrier((line, wgrad))
    wgrad = lax.all_to_all(wgrad, NEAR, 0, 0)
    stacks = [line] + [from_ahead(line, "y", k) for k in range(1, n_y)]
    wgrad = call(spread_sum, shape((far, rows, 128), BF16), 0, 1, size=1 << 19)(wgrad)
    wgrad = lax.all_to_all(wgrad, FAR, 0, 0, axis_index_groups=[led_by(far * 10 // 16, far)])
    feat_grad = call(
        gradient,
        shape((nodes, width), BF16),
        3,
        2 + n_y,
        scratch=[pltpu.VMEM((nodes, width), F32), pltpu.VMEM((parts, nodes, width), BF16)],
        flops=2 * count * tile * tile * width,
        size=3 << 20,
    )(src_tile, ahead, dst_tile, adjacency, base, *stacks)
    wgrad, feat_grad = lax.optimization_barrier((wgrad, feat_grad))
    wgrad = call(spread_sum, shape((near, rows, 128), BF16), 0, 1, size=1 << 19)(wgrad)
    wgrad = lax.all_to_all(wgrad, NEAR, 0, 0)

    def last(in_ref, out_ref):
        unpack(in_ref, out_ref, scale=1.0 / math.sqrt(total_nodes))

    weight_grads = call(last, shape((2, width, width), F32), 0, 1, size=1 << 20)(wgrad)
    return (output, feat_grad, weight_grads)


def solution(mesh):
    dom, grp = mesh.devices.shape
    side = math.isqrt(dom)
    fine = Mesh(
        mesh.devices.reshape(side, dom // side, grp // (2 * Z_LO), Z_LO, 2), ALL
    )
    rows = P(ALL, None)
    in_specs = (rows, P(ALL, None, None), P(ALL), rows, P(ALL), P(), P(), rows)
    out_specs = (rows, rows, P())
    return jax.shard_map(body, mesh=fine, in_specs=in_specs, out_specs=out_specs, check_vma=False)
```

```python
import functools
import math

import jax
import jax.numpy as jnp
from jax import lax
from jax.experimental import pallas as pl
from jax.experimental.pallas import tpu as pltpu
from jax.sharding import Mesh
from jax.sharding import PartitionSpec as P

F32 = jnp.float32
BF16 = jnp.bfloat16
Z_LO = 2
LINE = ("y", "x")
PLANE = ("y", "x", "core")
NEAR = ("y", "x", "z_lo", "core")
FAR = "z_hi"
ALL = ("y", "x", "z_hi", "z_lo", "core")
TN = (((0,), (0,)), ((), ()))
NT = (((1,), (1,)), ((), ()))
LIMIT = 32 * 1024 * 1024


def smem():
    return pl.BlockSpec(memory_space=pltpu.SMEM)


def vmem():
    return pl.BlockSpec(memory_space=pltpu.VMEM)


def call(kernel, outs, n_smem, n_vmem, scratch=(), flops=0, size=0):
    return pl.pallas_call(
        kernel,
        out_shape=outs,
        in_specs=[smem()] * n_smem + [vmem()] * n_vmem,
        out_specs=jax.tree.map(lambda _: vmem(), outs),
        scratch_shapes=list(scratch),
        compiler_params=pltpu.CompilerParams(vmem_limit_bytes=LIMIT),
        cost_estimate=pl.CostEstimate(flops=flops, bytes_accessed=size, transcendentals=0),
    )


def shape(dims, dtype):
    return jax.ShapeDtypeStruct(dims, dtype)


def partial_sums(
    src_in, peer_in, dst_in, feat_in, adj_in, out_ref, src_ref, peer_ref, dst_ref, feat_ref, adj_ref, sems, *, lead
):
    parts = out_ref.shape[0]
    pairs = ((src_in, src_ref), (peer_in, peer_ref), (dst_in, dst_ref), (feat_in, feat_ref), (adj_in, adj_ref))
    copies = [pltpu.make_async_copy(a, b, sems.at[k]) for k, (a, b) in enumerate(pairs)]
    for copy in reversed(copies):
        copy.start()
    count, tile, _ = adj_ref.shape
    out_ref[...] = jnp.zeros_like(out_ref)
    for copy in copies:
        copy.wait()
    for t in range(count):
        src = pl.multiple_of(src_ref[t] * tile, tile)
        dst = pl.multiple_of(dst_ref[t] * tile, tile)
        prod = jnp.dot(adj_ref[t], feat_ref[pl.ds(src, tile), :], preferred_element_type=F32)
        where = (lax.rem(peer_ref[t] + (parts - lead), parts), pl.ds(dst, tile), slice(None))
        out_ref[where] = (out_ref[where].astype(F32) + prod.astype(BF16).astype(F32)).astype(BF16)


def layer(recv_ref, feat_ref, ws_ref, wn_ref, grad_ref, out_ref, base_ref, agg_grad_ref, wg_ref):
    peers, nodes, width = recv_ref.shape
    agg = recv_ref[0].astype(F32)
    for p in range(1, peers):
        agg = agg + recv_ref[p].astype(F32)
    low = agg.astype(BF16)
    feat = feat_ref[...]
    pre = jnp.dot(feat, ws_ref[...], preferred_element_type=F32) + jnp.dot(
        low, wn_ref[...], preferred_element_type=F32
    )
    sig = jax.nn.sigmoid(pre)
    out_ref[...] = (pre * sig).astype(BF16)
    dpre = (grad_ref[...].astype(F32) * sig * (1.0 + pre * (1.0 - sig))).astype(BF16)
    agg_grad = lax.dot_general(dpre, wn_ref[...], NT, preferred_element_type=F32).astype(BF16)
    for x in range(agg_grad_ref.shape[0]):
        agg_grad_ref[x] = agg_grad
    chunks, rows, lanes = wg_ref.shape
    half = chunks // 2
    for k, left in enumerate((feat, low)):
        part = lax.dot_general(left, dpre, TN, preferred_element_type=F32)
        part = part.reshape(half, rows // 2, width)
        part = jnp.concatenate([part[:, :, :lanes], part[:, :, lanes:]], axis=1)
        wg_ref[k * half : (k + 1) * half] = part.astype(BF16)
    base_ref[...] = lax.dot_general(dpre, ws_ref[...], NT, preferred_element_type=F32)


def gradient(
    src_ref, peer_ref, dst_ref, adj_ref, base_ref, s0, s1, s2, s3, out_ref, acc_ref, every_ref
):
    count, tile, _ = adj_ref.shape
    wide = s0.shape[0]
    for k, stack in enumerate((s0, s1, s2, s3)):
        every_ref[k * wide : (k + 1) * wide] = stack[...]
    acc_ref[...] = base_ref[...]
    for t in range(count):
        src = pl.multiple_of(src_ref[t] * tile, tile)
        dst = pl.multiple_of(dst_ref[t] * tile, tile)
        picked = every_ref[peer_ref[t], pl.ds(dst, tile), :]
        acc_ref[pl.ds(src, tile), :] += lax.dot_general(
            adj_ref[t], picked, TN, preferred_element_type=F32
        )
    out_ref[...] = acc_ref[...].astype(BF16)


def spread_sum(in_ref, out_ref):
    total = jnp.sum(in_ref[...].astype(F32), axis=0).astype(out_ref.dtype)
    for p in range(out_ref.shape[0]):
        out_ref[p] = total


def unpack(in_ref, out_ref, *, scale):
    got = in_ref[...].astype(F32) * scale
    chunks, rows, lanes = got.shape
    got = jnp.concatenate([got[:, : rows // 2], got[:, rows // 2 :]], axis=2)
    out_ref[...] = got.reshape(out_ref.shape)


def led_by(first, count):
    return [(first + k) % count for k in range(count)]


def in_plane(side):
    return lambda y, x, core: (y % side * side + x % side) * 2 + core


def first_lines(side):
    at, each = in_plane(side), range(side)
    return [[at(y, x, 0) for x in each] for y in each] + [[at(y, x, 1) for y in each] for x in each]


def from_ahead(value, side, step):
    at, each = in_plane(side), range(side)
    pairs = [(at(y + step, x, 0), at(y, x, 0)) for y in each for x in each]
    pairs += [(at(y, x + step, 1), at(y, x, 1)) for y in each for x in each]
    return lax.ppermute(value, PLANE, pairs)


def body(features, adjacency, src_tile, dst_peer, dst_tile, w_self, w_neigh, out_grad):
    nodes, width = features.shape
    count, tile, _ = adjacency.shape
    parts = lax.axis_size(LINE)
    near, far = lax.axis_size(NEAR), lax.axis_size(FAR)
    total_nodes = nodes * lax.axis_size(ALL)
    rows = 2 * width * width // near // 128
    peer = dst_peer.reshape(count)
    lead = parts * 10 // 16
    side = math.isqrt(parts)
    peer_y, peer_x = peer // side, peer % side
    ahead = jnp.where(
        lax.axis_index("core") == 0,
        (peer_y - lax.axis_index("y")) % side * side + peer_x,
        (peer_x - lax.axis_index("x")) % side * side + peer_y,
    )
    dense = pl.pallas_call(
        functools.partial(partial_sums, lead=lead),
        out_shape=shape((parts, nodes, width), BF16),
        in_specs=[pl.BlockSpec(memory_space=pltpu.HBM)] * 5,
        out_specs=vmem(),
        scratch_shapes=[pltpu.SMEM((count,), jnp.int32)] * 3
        + [pltpu.VMEM((nodes, width), BF16), pltpu.VMEM((count, tile, tile), BF16)]
        + [pltpu.SemaphoreType.DMA((5,))],
        compiler_params=pltpu.CompilerParams(vmem_limit_bytes=60 << 20),
        cost_estimate=pl.CostEstimate(
            flops=2 * count * tile * tile * width, bytes_accessed=3 << 20, transcendentals=0
        ),
    )(src_tile, peer, dst_tile, features, adjacency)
    recv = lax.all_to_all(dense, LINE, 0, 0, axis_index_groups=[led_by(lead, parts)])
    output, base, line, wgrad = call(
        layer,
        (
            shape((nodes, width), BF16),
            shape((nodes, width), F32),
            shape((side, nodes, width), BF16),
            shape((near, rows, 128), BF16),
        ),
        0,
        5,
        flops=12 * nodes * width * width,
        size=5 << 20,
    )(recv, features, w_self, w_neigh, out_grad)
    line = lax.all_to_all(line, PLANE, 0, 0, axis_index_groups=first_lines(side))
    line, wgrad = lax.optimization_barrier((line, wgrad))
    wgrad = lax.all_to_all(wgrad, NEAR, 0, 0)
    stacks = [line] + [from_ahead(line, side, k) for k in range(1, side)]
    wgrad = call(spread_sum, shape((far, rows, 128), BF16), 0, 1, size=1 << 19)(wgrad)
    wgrad = lax.all_to_all(wgrad, FAR, 0, 0, axis_index_groups=[led_by(far * 10 // 16, far)])
    feat_grad = call(
        gradient,
        shape((nodes, width), BF16),
        3,
        2 + side,
        scratch=[pltpu.VMEM((nodes, width), F32), pltpu.VMEM((parts, nodes, width), BF16)],
        flops=2 * count * tile * tile * width,
        size=3 << 20,
    )(src_tile, ahead, dst_tile, adjacency, base, *stacks)
    wgrad, feat_grad = lax.optimization_barrier((wgrad, feat_grad))
    wgrad = call(spread_sum, shape((near, rows, 128), BF16), 0, 1, size=1 << 19)(wgrad)
    wgrad = lax.all_to_all(wgrad, NEAR, 0, 0)

    def last(in_ref, out_ref):
        unpack(in_ref, out_ref, scale=1.0 / math.sqrt(total_nodes))

    weight_grads = call(last, shape((2, width, width), F32), 0, 1, size=1 << 20)(wgrad)
    return (output, feat_grad, weight_grads)


def solution(mesh):
    dom, grp = mesh.devices.shape
    side = math.isqrt(dom)
    fine = Mesh(
        mesh.devices.reshape(side, dom // side, grp // (2 * Z_LO), Z_LO, 2), ALL
    )
    rows = P(ALL, None)
    in_specs = (rows, P(ALL, None, None), P(ALL), rows, P(ALL), P(), P(), rows)
    out_specs = (rows, rows, P())
    return jax.shard_map(body, mesh=fine, in_specs=in_specs, out_specs=out_specs, check_vma=False)
```

```python
import functools
import math

import jax
import jax.numpy as jnp
from jax import lax
from jax.experimental import pallas as pl
from jax.experimental.pallas import tpu as pltpu
from jax.sharding import Mesh
from jax.sharding import PartitionSpec as P

F32 = jnp.float32
BF16 = jnp.bfloat16
Z_LO = 2
LINE = ("y", "x")
PLANE = ("y", "x", "core")
NEAR = ("y", "x", "z_lo", "core")
FAR = "z_hi"
ALL = ("y", "x", "z_hi", "z_lo", "core")
TN = (((0,), (0,)), ((), ()))
NT = (((1,), (1,)), ((), ()))
LIMIT = 32 * 1024 * 1024


def smem():
    return pl.BlockSpec(memory_space=pltpu.SMEM)


def vmem():
    return pl.BlockSpec(memory_space=pltpu.VMEM)


def call(kernel, outs, n_smem, n_vmem, scratch=(), flops=0, size=0):
    return pl.pallas_call(
        kernel,
        out_shape=outs,
        in_specs=[smem()] * n_smem + [vmem()] * n_vmem,
        out_specs=jax.tree.map(lambda _: vmem(), outs),
        scratch_shapes=list(scratch),
        compiler_params=pltpu.CompilerParams(vmem_limit_bytes=LIMIT),
        cost_estimate=pl.CostEstimate(flops=flops, bytes_accessed=size, transcendentals=0),
    )


def shape(dims, dtype):
    return jax.ShapeDtypeStruct(dims, dtype)


def partial_sums(
    src_in, peer_in, dst_in, feat_in, adj_in, out_ref, src_ref, peer_ref, dst_ref, feat_ref, adj_ref, sems, *, lead
):
    parts = out_ref.shape[0]
    pairs = ((src_in, src_ref), (peer_in, peer_ref), (dst_in, dst_ref), (feat_in, feat_ref), (adj_in, adj_ref))
    copies = [pltpu.make_async_copy(a, b, sems.at[k]) for k, (a, b) in enumerate(pairs)]
    for copy in reversed(copies):
        copy.start()
    count, tile, _ = adj_ref.shape
    out_ref[...] = jnp.zeros_like(out_ref)
    for copy in copies:
        copy.wait()
    for t in range(count):
        src = pl.multiple_of(src_ref[t] * tile, tile)
        dst = pl.multiple_of(dst_ref[t] * tile, tile)
        prod = jnp.dot(adj_ref[t], feat_ref[pl.ds(src, tile), :], preferred_element_type=F32)
        where = (lax.rem(peer_ref[t] + (parts - lead), parts), pl.ds(dst, tile), slice(None))
        out_ref[where] = (out_ref[where].astype(F32) + prod.astype(BF16).astype(F32)).astype(BF16)


def layer(recv_ref, feat_ref, ws_ref, wn_ref, grad_ref, out_ref, base_ref, agg_grad_ref, wg_ref):
    peers, nodes, width = recv_ref.shape
    agg = recv_ref[0].astype(F32)
    for p in range(1, peers):
        agg = agg + recv_ref[p].astype(F32)
    low = agg.astype(BF16)
    feat = feat_ref[...]
    pre = jnp.dot(feat, ws_ref[...], preferred_element_type=F32) + jnp.dot(
        low, wn_ref[...], preferred_element_type=F32
    )
    sig = jax.nn.sigmoid(pre)
    out_ref[...] = (pre * sig).astype(BF16)
    dpre = (grad_ref[...].astype(F32) * sig * (1.0 + pre * (1.0 - sig))).astype(BF16)
    agg_grad = lax.dot_general(dpre, wn_ref[...], NT, preferred_element_type=F32).astype(BF16)
    for x in range(agg_grad_ref.shape[0]):
        agg_grad_ref[x] = agg_grad
    chunks, rows, lanes = wg_ref.shape
    half = chunks // 2
    for k, left in enumerate((feat, low)):
        part = lax.dot_general(left, dpre, TN, preferred_element_type=F32)
        part = part.reshape(half, rows // 2, width)
        part = jnp.concatenate([part[:, :, :lanes], part[:, :, lanes:]], axis=1)
        wg_ref[k * half : (k + 1) * half] = part.astype(BF16)
    base_ref[...] = lax.dot_general(dpre, ws_ref[...], NT, preferred_element_type=F32)


def gradient(
    src_ref, peer_ref, dst_ref, adj_ref, base_ref, s0, s1, s2, s3, out_ref, acc_ref, every_ref
):
    count, tile, _ = adj_ref.shape
    wide = s0.shape[0]
    for k, stack in enumerate((s0, s1, s2, s3)):
        every_ref[k * wide : (k + 1) * wide] = stack[...]
    acc_ref[...] = base_ref[...]
    for t in range(count):
        src = pl.multiple_of(src_ref[t] * tile, tile)
        dst = pl.multiple_of(dst_ref[t] * tile, tile)
        picked = every_ref[peer_ref[t], pl.ds(dst, tile), :]
        acc_ref[pl.ds(src, tile), :] += lax.dot_general(
            adj_ref[t], picked, TN, preferred_element_type=F32
        )
    out_ref[...] = acc_ref[...].astype(BF16)


def spread_sum(in_ref, out_ref):
    total = jnp.sum(in_ref[...].astype(F32), axis=0).astype(out_ref.dtype)
    for p in range(out_ref.shape[0]):
        out_ref[p] = total


def unpack(in_ref, out_ref, *, scale):
    got = in_ref[...].astype(F32) * scale
    chunks, rows, lanes = got.shape
    got = jnp.concatenate([got[:, : rows // 2], got[:, rows // 2 :]], axis=2)
    out_ref[...] = got.reshape(out_ref.shape)


def led_by(first, count):
    return [(first + k) % count for k in range(count)]


def in_plane(side):
    return lambda y, x, core: (y % side * side + x % side) * 2 + core


def first_lines(side):
    at, each = in_plane(side), range(side)
    return [[at(y, x, 0) for x in each] for y in each] + [[at(y, x, 1) for y in each] for x in each]


def from_ahead(value, side, step):
    at, each = in_plane(side), range(side)
    pairs = [(at(y + step, x, 0), at(y, x, 0)) for y in each for x in each]
    pairs += [(at(y, x + step, 1), at(y, x, 1)) for y in each for x in each]
    return lax.ppermute(value, PLANE, pairs)


def body(features, adjacency, src_tile, dst_peer, dst_tile, w_self, w_neigh, out_grad):
    nodes, width = features.shape
    count, tile, _ = adjacency.shape
    parts = lax.axis_size(LINE)
    near, far = lax.axis_size(NEAR), lax.axis_size(FAR)
    total_nodes = nodes * lax.axis_size(ALL)
    rows = 2 * width * width // near // 128
    peer = dst_peer.reshape(count)
    lead = parts * 10 // 16
    side = math.isqrt(parts)
    peer_y, peer_x = peer // side, peer % side
    ahead = jnp.where(
        lax.axis_index("core") == 0,
        (peer_y - lax.axis_index("y")) % side * side + peer_x,
        (peer_x - lax.axis_index("x")) % side * side + peer_y,
    )
    dense = pl.pallas_call(
        functools.partial(partial_sums, lead=lead),
        out_shape=shape((parts, nodes, width), BF16),
        in_specs=[pl.BlockSpec(memory_space=pltpu.HBM)] * 5,
        out_specs=vmem(),
        scratch_shapes=[pltpu.SMEM((count,), jnp.int32)] * 3
        + [pltpu.VMEM((nodes, width), BF16), pltpu.VMEM((count, tile, tile), BF16)]
        + [pltpu.SemaphoreType.DMA((5,))],
        compiler_params=pltpu.CompilerParams(vmem_limit_bytes=60 << 20),
        cost_estimate=pl.CostEstimate(
            flops=2 * count * tile * tile * width, bytes_accessed=3 << 20, transcendentals=0
        ),
    )(src_tile, peer, dst_tile, features, adjacency)
    recv = lax.all_to_all(dense, LINE, 0, 0, axis_index_groups=[led_by(lead, parts)])
    output, base, line, wgrad = call(
        layer,
        (
            shape((nodes, width), BF16),
            shape((nodes, width), F32),
            shape((side, nodes, width), BF16),
            shape((near, rows, 128), BF16),
        ),
        0,
        5,
        flops=12 * nodes * width * width,
        size=5 << 20,
    )(recv, features, w_self, w_neigh, out_grad)
    line = lax.all_to_all(line, PLANE, 0, 0, axis_index_groups=first_lines(side))
    line, wgrad = lax.optimization_barrier((line, wgrad))
    wgrad = lax.all_to_all(wgrad, NEAR, 0, 0, axis_index_groups=[led_by(near * 10 // 16, near)])
    stacks = [line] + [from_ahead(line, side, k) for k in range(1, side)]
    wgrad = call(spread_sum, shape((far, rows, 128), BF16), 0, 1, size=1 << 19)(wgrad)
    wgrad = lax.all_to_all(wgrad, FAR, 0, 0, axis_index_groups=[led_by(far * 10 // 16, far)])
    feat_grad = call(
        gradient,
        shape((nodes, width), BF16),
        3,
        2 + side,
        scratch=[pltpu.VMEM((nodes, width), F32), pltpu.VMEM((parts, nodes, width), BF16)],
        flops=2 * count * tile * tile * width,
        size=3 << 20,
    )(src_tile, ahead, dst_tile, adjacency, base, *stacks)
    wgrad, feat_grad = lax.optimization_barrier((wgrad, feat_grad))
    wgrad = call(spread_sum, shape((near, rows, 128), BF16), 0, 1, size=1 << 19)(wgrad)
    wgrad = lax.all_to_all(wgrad, NEAR, 0, 0, axis_index_groups=[led_by(near * 10 // 16, near)])

    def last(in_ref, out_ref):
        unpack(in_ref, out_ref, scale=1.0 / math.sqrt(total_nodes))

    weight_grads = call(last, shape((2, width, width), F32), 0, 1, size=1 << 20)(wgrad)
    return (output, feat_grad, weight_grads)


def solution(mesh):
    dom, grp = mesh.devices.shape
    side = math.isqrt(dom)
    fine = Mesh(
        mesh.devices.reshape(side, dom // side, grp // (2 * Z_LO), Z_LO, 2), ALL
    )
    rows = P(ALL, None)
    in_specs = (rows, P(ALL, None, None), P(ALL), rows, P(ALL), P(), P(), rows)
    out_specs = (rows, rows, P())
    return jax.shard_map(body, mesh=fine, in_specs=in_specs, out_specs=out_specs, check_vma=False)
```

```python
import functools
import math

import jax
import jax.numpy as jnp
from jax import lax
from jax.experimental import pallas as pl
from jax.experimental.pallas import tpu as pltpu
from jax.sharding import Mesh
from jax.sharding import PartitionSpec as P

F32 = jnp.float32
BF16 = jnp.bfloat16
Z_LO = 2
LINE = ("y", "x")
PLANE = ("y", "x", "core")
NEAR = ("y", "x", "z_lo", "core")
FAR = "z_hi"
ALL = ("y", "x", "z_hi", "z_lo", "core")
TN = (((0,), (0,)), ((), ()))
NT = (((1,), (1,)), ((), ()))
LIMIT = 32 * 1024 * 1024


def smem():
    return pl.BlockSpec(memory_space=pltpu.SMEM)


def vmem():
    return pl.BlockSpec(memory_space=pltpu.VMEM)


def call(kernel, outs, n_smem, n_vmem, scratch=(), flops=0, size=0):
    return pl.pallas_call(
        kernel,
        out_shape=outs,
        in_specs=[smem()] * n_smem + [vmem()] * n_vmem,
        out_specs=jax.tree.map(lambda _: vmem(), outs),
        scratch_shapes=list(scratch),
        compiler_params=pltpu.CompilerParams(vmem_limit_bytes=LIMIT),
        cost_estimate=pl.CostEstimate(flops=flops, bytes_accessed=size, transcendentals=0),
    )


def shape(dims, dtype):
    return jax.ShapeDtypeStruct(dims, dtype)


def partial_sums(
    src_in, peer_in, dst_in, feat_in, adj_in, out_ref, src_ref, peer_ref, dst_ref, feat_ref, adj_ref, sems, *, lead
):
    parts = out_ref.shape[0]
    pairs = ((src_in, src_ref), (peer_in, peer_ref), (dst_in, dst_ref), (feat_in, feat_ref), (adj_in, adj_ref))
    copies = [pltpu.make_async_copy(a, b, sems.at[k]) for k, (a, b) in enumerate(pairs)]
    for copy in reversed(copies):
        copy.start()
    count, tile, _ = adj_ref.shape
    out_ref[...] = jnp.zeros_like(out_ref)
    for copy in copies:
        copy.wait()
    for t in range(count):
        src = pl.multiple_of(src_ref[t] * tile, tile)
        dst = pl.multiple_of(dst_ref[t] * tile, tile)
        prod = jnp.dot(adj_ref[t], feat_ref[pl.ds(src, tile), :], preferred_element_type=F32)
        where = (lax.rem(peer_ref[t] + (parts - lead), parts), pl.ds(dst, tile), slice(None))
        out_ref[where] = (out_ref[where].astype(F32) + prod.astype(BF16).astype(F32)).astype(BF16)


def layer(recv_ref, feat_ref, ws_ref, wn_ref, grad_ref, out_ref, base_ref, agg_grad_ref, wg_ref):
    peers, nodes, width = recv_ref.shape
    agg = recv_ref[0].astype(F32)
    for p in range(1, peers):
        agg = agg + recv_ref[p].astype(F32)
    low = agg.astype(BF16)
    feat = feat_ref[...]
    pre = jnp.dot(feat, ws_ref[...], preferred_element_type=F32) + jnp.dot(
        low, wn_ref[...], preferred_element_type=F32
    )
    sig = jax.nn.sigmoid(pre)
    out_ref[...] = (pre * sig).astype(BF16)
    dpre = (grad_ref[...].astype(F32) * sig * (1.0 + pre * (1.0 - sig))).astype(BF16)
    agg_grad = lax.dot_general(dpre, wn_ref[...], NT, preferred_element_type=F32).astype(BF16)
    for x in range(agg_grad_ref.shape[0]):
        agg_grad_ref[x] = agg_grad
    chunks, rows, lanes = wg_ref.shape
    half = chunks // 2
    for k, left in enumerate((feat, low)):
        part = lax.dot_general(left, dpre, TN, preferred_element_type=F32)
        part = part.reshape(half, rows // 2, width)
        part = jnp.concatenate([part[:, :, :lanes], part[:, :, lanes:]], axis=1)
        wg_ref[k * half : (k + 1) * half] = part.astype(BF16)
    base_ref[...] = lax.dot_general(dpre, ws_ref[...], NT, preferred_element_type=F32)


def gradient(
    src_ref, peer_ref, dst_ref, adj_ref, base_ref, s0, s1, s2, s3, out_ref, acc_ref, every_ref
):
    count, tile, _ = adj_ref.shape
    wide = s0.shape[0]
    for k, stack in enumerate((s0, s1, s2, s3)):
        every_ref[k * wide : (k + 1) * wide] = stack[...]
    acc_ref[...] = base_ref[...]
    for t in range(count):
        src = pl.multiple_of(src_ref[t] * tile, tile)
        dst = pl.multiple_of(dst_ref[t] * tile, tile)
        picked = every_ref[peer_ref[t], pl.ds(dst, tile), :]
        acc_ref[pl.ds(src, tile), :] += lax.dot_general(
            adj_ref[t], picked, TN, preferred_element_type=F32
        )
    out_ref[...] = acc_ref[...].astype(BF16)


def spread_sum(in_ref, out_ref):
    total = jnp.sum(in_ref[...].astype(F32), axis=0).astype(out_ref.dtype)
    for p in range(out_ref.shape[0]):
        out_ref[p] = total


def unpack(in_ref, out_ref, *, scale):
    got = in_ref[...].astype(F32) * scale
    chunks, rows, lanes = got.shape
    got = jnp.concatenate([got[:, : rows // 2], got[:, rows // 2 :]], axis=2)
    out_ref[...] = got.reshape(out_ref.shape)


def led_by(first, count):
    return [(first + k) % count for k in range(count)]


def in_plane(side):
    return lambda y, x, core: (y % side * side + x % side) * 2 + core


def first_lines(side):
    at, each, led = in_plane(side), range(side), led_by(side // 2, side)
    return [[at(y, x, 0) for x in led] for y in each] + [[at(y, x, 1) for y in led] for x in each]


def from_ahead(value, side, step):
    at, each = in_plane(side), range(side)
    pairs = [(at(y + step, x, 0), at(y, x, 0)) for y in each for x in each]
    pairs += [(at(y, x + step, 1), at(y, x, 1)) for y in each for x in each]
    return lax.ppermute(value, PLANE, pairs)


def body(features, adjacency, src_tile, dst_peer, dst_tile, w_self, w_neigh, out_grad):
    nodes, width = features.shape
    count, tile, _ = adjacency.shape
    parts = lax.axis_size(LINE)
    near, far = lax.axis_size(NEAR), lax.axis_size(FAR)
    total_nodes = nodes * lax.axis_size(ALL)
    rows = 2 * width * width // near // 128
    peer = dst_peer.reshape(count)
    lead = parts * 10 // 16
    side = math.isqrt(parts)
    peer_y, peer_x = peer // side, peer % side
    ahead = jnp.where(
        lax.axis_index("core") == 0,
        (peer_y - lax.axis_index("y")) % side * side + (peer_x - side // 2) % side,
        (peer_x - lax.axis_index("x")) % side * side + (peer_y - side // 2) % side,
    )
    dense = pl.pallas_call(
        functools.partial(partial_sums, lead=lead),
        out_shape=shape((parts, nodes, width), BF16),
        in_specs=[pl.BlockSpec(memory_space=pltpu.HBM)] * 5,
        out_specs=vmem(),
        scratch_shapes=[pltpu.SMEM((count,), jnp.int32)] * 3
        + [pltpu.VMEM((nodes, width), BF16), pltpu.VMEM((count, tile, tile), BF16)]
        + [pltpu.SemaphoreType.DMA((5,))],
        compiler_params=pltpu.CompilerParams(vmem_limit_bytes=60 << 20),
        cost_estimate=pl.CostEstimate(
            flops=2 * count * tile * tile * width, bytes_accessed=3 << 20, transcendentals=0
        ),
    )(src_tile, peer, dst_tile, features, adjacency)
    recv = lax.all_to_all(dense, LINE, 0, 0, axis_index_groups=[led_by(lead, parts)])
    output, base, line, wgrad = call(
        layer,
        (
            shape((nodes, width), BF16),
            shape((nodes, width), F32),
            shape((side, nodes, width), BF16),
            shape((near, rows, 128), BF16),
        ),
        0,
        5,
        flops=12 * nodes * width * width,
        size=5 << 20,
    )(recv, features, w_self, w_neigh, out_grad)
    line = lax.all_to_all(line, PLANE, 0, 0, axis_index_groups=first_lines(side))
    line, wgrad = lax.optimization_barrier((line, wgrad))
    wgrad = lax.all_to_all(wgrad, NEAR, 0, 0, axis_index_groups=[led_by(near * 10 // 16, near)])
    stacks = [line] + [from_ahead(line, side, k) for k in range(1, side)]
    wgrad = call(spread_sum, shape((far, rows, 128), BF16), 0, 1, size=1 << 19)(wgrad)
    wgrad = lax.all_to_all(wgrad, FAR, 0, 0, axis_index_groups=[led_by(far * 10 // 16, far)])
    feat_grad = call(
        gradient,
        shape((nodes, width), BF16),
        3,
        2 + side,
        scratch=[pltpu.VMEM((nodes, width), F32), pltpu.VMEM((parts, nodes, width), BF16)],
        flops=2 * count * tile * tile * width,
        size=3 << 20,
    )(src_tile, ahead, dst_tile, adjacency, base, *stacks)
    wgrad, feat_grad = lax.optimization_barrier((wgrad, feat_grad))
    wgrad = call(spread_sum, shape((near, rows, 128), BF16), 0, 1, size=1 << 19)(wgrad)
    wgrad = lax.all_to_all(wgrad, NEAR, 0, 0, axis_index_groups=[led_by(near * 10 // 16, near)])

    def last(in_ref, out_ref):
        unpack(in_ref, out_ref, scale=1.0 / math.sqrt(total_nodes))

    weight_grads = call(last, shape((2, width, width), F32), 0, 1, size=1 << 20)(wgrad)
    return (output, feat_grad, weight_grads)


def solution(mesh):
    dom, grp = mesh.devices.shape
    side = math.isqrt(dom)
    fine = Mesh(
        mesh.devices.reshape(side, dom // side, grp // (2 * Z_LO), Z_LO, 2), ALL
    )
    rows = P(ALL, None)
    in_specs = (rows, P(ALL, None, None), P(ALL), rows, P(ALL), P(), P(), rows)
    out_specs = (rows, rows, P())
    return jax.shard_map(body, mesh=fine, in_specs=in_specs, out_specs=out_specs, check_vma=False)
```

```python
import functools
import math

import jax
import jax.numpy as jnp
from jax import lax
from jax.experimental import pallas as pl
from jax.experimental.pallas import tpu as pltpu
from jax.sharding import Mesh
from jax.sharding import PartitionSpec as P

F32 = jnp.float32
BF16 = jnp.bfloat16
Z_LO = 2
LINE = ("y", "x")
PLANE = ("y", "x", "core")
NEAR = ("y", "x", "z_lo", "core")
FAR = "z_hi"
ALL = ("y", "x", "z_hi", "z_lo", "core")
TN = (((0,), (0,)), ((), ()))
NT = (((1,), (1,)), ((), ()))
LIMIT = 32 * 1024 * 1024


def smem():
    return pl.BlockSpec(memory_space=pltpu.SMEM)


def vmem():
    return pl.BlockSpec(memory_space=pltpu.VMEM)


def call(kernel, outs, n_smem, n_vmem, scratch=(), flops=0, size=0):
    return pl.pallas_call(
        kernel,
        out_shape=outs,
        in_specs=[smem()] * n_smem + [vmem()] * n_vmem,
        out_specs=jax.tree.map(lambda _: vmem(), outs),
        scratch_shapes=list(scratch),
        compiler_params=pltpu.CompilerParams(vmem_limit_bytes=LIMIT),
        cost_estimate=pl.CostEstimate(flops=flops, bytes_accessed=size, transcendentals=0),
    )


def shape(dims, dtype):
    return jax.ShapeDtypeStruct(dims, dtype)


def partial_sums(
    src_in, peer_in, dst_in, feat_in, adj_in, out_ref, src_ref, peer_ref, dst_ref, feat_ref, adj_ref, sems, *, lead
):
    parts = out_ref.shape[0]
    pairs = ((src_in, src_ref), (peer_in, peer_ref), (dst_in, dst_ref), (feat_in, feat_ref), (adj_in, adj_ref))
    copies = [pltpu.make_async_copy(a, b, sems.at[k]) for k, (a, b) in enumerate(pairs)]
    for copy in reversed(copies):
        copy.start()
    count, tile, _ = adj_ref.shape
    out_ref[...] = jnp.zeros_like(out_ref)
    for copy in copies:
        copy.wait()
    for t in range(count):
        src = pl.multiple_of(src_ref[t] * tile, tile)
        dst = pl.multiple_of(dst_ref[t] * tile, tile)
        prod = jnp.dot(adj_ref[t], feat_ref[pl.ds(src, tile), :], preferred_element_type=F32)
        where = (lax.rem(peer_ref[t] + (parts - lead), parts), pl.ds(dst, tile), slice(None))
        out_ref[where] = (out_ref[where].astype(F32) + prod.astype(BF16).astype(F32)).astype(BF16)


def layer(recv_ref, feat_ref, ws_ref, wn_ref, grad_ref, out_ref, base_ref, agg_grad_ref, wg_ref):
    peers, nodes, width = recv_ref.shape
    agg = recv_ref[0].astype(F32)
    for p in range(1, peers):
        agg = agg + recv_ref[p].astype(F32)
    low = agg.astype(BF16)
    feat = feat_ref[...]
    pre = jnp.dot(feat, ws_ref[...], preferred_element_type=F32) + jnp.dot(
        low, wn_ref[...], preferred_element_type=F32
    )
    sig = jax.nn.sigmoid(pre)
    out_ref[...] = (pre * sig).astype(BF16)
    dpre = (grad_ref[...].astype(F32) * sig * (1.0 + pre * (1.0 - sig))).astype(BF16)
    agg_grad = lax.dot_general(dpre, wn_ref[...], NT, preferred_element_type=F32).astype(BF16)
    for x in range(agg_grad_ref.shape[0]):
        agg_grad_ref[x] = agg_grad
    chunks, rows, lanes = wg_ref.shape
    half = chunks // 2
    for k, left in enumerate((feat, low)):
        part = lax.dot_general(left, dpre, TN, preferred_element_type=F32)
        part = part.reshape(half, rows // 2, width)
        part = jnp.concatenate([part[:, :, :lanes], part[:, :, lanes:]], axis=1)
        wg_ref[k * half : (k + 1) * half] = part.astype(BF16)
    base_ref[...] = lax.dot_general(dpre, ws_ref[...], NT, preferred_element_type=F32)


def gradient(
    src_ref, peer_ref, dst_ref, adj_ref, base_ref, s0, s1, s2, s3, out_ref, acc_ref, every_ref
):
    count, tile, _ = adj_ref.shape
    wide = s0.shape[0]
    for k, stack in enumerate((s0, s1, s2, s3)):
        every_ref[k * wide : (k + 1) * wide] = stack[...]
    acc_ref[...] = base_ref[...]
    for t in range(count):
        src = pl.multiple_of(src_ref[t] * tile, tile)
        dst = pl.multiple_of(dst_ref[t] * tile, tile)
        picked = every_ref[peer_ref[t], pl.ds(dst, tile), :]
        acc_ref[pl.ds(src, tile), :] += lax.dot_general(
            adj_ref[t], picked, TN, preferred_element_type=F32
        )
    out_ref[...] = acc_ref[...].astype(BF16)


def spread_sum(in_ref, out_ref):
    total = jnp.sum(in_ref[...].astype(F32), axis=0).astype(out_ref.dtype)
    for p in range(out_ref.shape[0]):
        out_ref[p] = total


def unpack(in_ref, out_ref, *, scale):
    got = in_ref[...].astype(F32) * scale
    chunks, rows, lanes = got.shape
    got = jnp.concatenate([got[:, : rows // 2], got[:, rows // 2 :]], axis=2)
    out_ref[...] = got.reshape(out_ref.shape)


def led_by(first, count):
    return [(first + k) % count for k in range(count)]


def in_plane(side):
    return lambda y, x, core: (y % side * side + x % side) * 2 + core


def first_lines(side):
    at, each, led = in_plane(side), range(side), led_by(side // 2, side)
    return [[at(y, x, 0) for x in led] for y in each] + [[at(y, x, 1) for y in led] for x in each]


def from_ahead(value, side, step):
    at, each = in_plane(side), range(side)
    pairs = [(at(y + step, x, 0), at(y, x, 0)) for y in each for x in each]
    pairs += [(at(y, x + step, 1), at(y, x, 1)) for y in each for x in each]
    return lax.ppermute(value, PLANE, pairs)


def body(features, adjacency, src_tile, dst_peer, dst_tile, w_self, w_neigh, out_grad):
    nodes, width = features.shape
    count, tile, _ = adjacency.shape
    parts = lax.axis_size(LINE)
    near, far = lax.axis_size(NEAR), lax.axis_size(FAR)
    total_nodes = nodes * lax.axis_size(ALL)
    rows = 2 * width * width // near // 128
    peer = dst_peer.reshape(count)
    lead = parts * 10 // 16
    side = math.isqrt(parts)
    peer_y, peer_x = peer // side, peer % side
    ahead = jnp.where(
        lax.axis_index("core") == 0,
        (peer_y - lax.axis_index("y")) % side * side + (peer_x - side // 2) % side,
        (peer_x - lax.axis_index("x")) % side * side + (peer_y - side // 2) % side,
    )
    dense = pl.pallas_call(
        functools.partial(partial_sums, lead=lead),
        out_shape=shape((parts, nodes, width), BF16),
        in_specs=[pl.BlockSpec(memory_space=pltpu.HBM)] * 5,
        out_specs=vmem(),
        scratch_shapes=[pltpu.SMEM((count,), jnp.int32)] * 3
        + [pltpu.VMEM((nodes, width), BF16), pltpu.VMEM((count, tile, tile), BF16)]
        + [pltpu.SemaphoreType.DMA((5,))],
        compiler_params=pltpu.CompilerParams(vmem_limit_bytes=60 << 20),
        cost_estimate=pl.CostEstimate(
            flops=2 * count * tile * tile * width, bytes_accessed=3 << 20, transcendentals=0
        ),
    )(src_tile, peer, dst_tile, features, adjacency)
    recv = lax.all_to_all(dense, LINE, 0, 0, axis_index_groups=[led_by(lead, parts)])
    output, base, line, wgrad = call(
        layer,
        (
            shape((nodes, width), BF16),
            shape((nodes, width), F32),
            shape((side, nodes, width), BF16),
            shape((near, rows, 128), BF16),
        ),
        0,
        5,
        flops=12 * nodes * width * width,
        size=5 << 20,
    )(recv, features, w_self, w_neigh, out_grad)
    line = lax.all_to_all(line, PLANE, 0, 0, axis_index_groups=first_lines(side))
    line, wgrad = lax.optimization_barrier((line, wgrad))
    wgrad = lax.all_to_all(wgrad, NEAR, 0, 0, axis_index_groups=[led_by(near * 11 // 16, near)])
    stacks = [line] + [from_ahead(line, side, k) for k in range(1, side)]
    wgrad = call(spread_sum, shape((far, rows, 128), BF16), 0, 1, size=1 << 19)(wgrad)
    wgrad = lax.all_to_all(wgrad, FAR, 0, 0, axis_index_groups=[led_by(far * 10 // 16, far)])
    feat_grad = call(
        gradient,
        shape((nodes, width), BF16),
        3,
        2 + side,
        scratch=[pltpu.VMEM((nodes, width), F32), pltpu.VMEM((parts, nodes, width), BF16)],
        flops=2 * count * tile * tile * width,
        size=3 << 20,
    )(src_tile, ahead, dst_tile, adjacency, base, *stacks)
    wgrad, feat_grad = lax.optimization_barrier((wgrad, feat_grad))
    wgrad = call(spread_sum, shape((near, rows, 128), BF16), 0, 1, size=1 << 19)(wgrad)
    wgrad = lax.all_to_all(wgrad, NEAR, 0, 0, axis_index_groups=[led_by(near * 11 // 16, near)])

    def last(in_ref, out_ref):
        unpack(in_ref, out_ref, scale=1.0 / math.sqrt(total_nodes))

    weight_grads = call(last, shape((2, width, width), F32), 0, 1, size=1 << 20)(wgrad)
    return (output, feat_grad, weight_grads)


def solution(mesh):
    dom, grp = mesh.devices.shape
    side = math.isqrt(dom)
    fine = Mesh(
        mesh.devices.reshape(side, dom // side, grp // (2 * Z_LO), Z_LO, 2), ALL
    )
    rows = P(ALL, None)
    in_specs = (rows, P(ALL, None, None), P(ALL), rows, P(ALL), P(), P(), rows)
    out_specs = (rows, rows, P())
    return jax.shard_map(body, mesh=fine, in_specs=in_specs, out_specs=out_specs, check_vma=False)
```
